32 devices in a mesh: dp: 8 (over z, y), seq: 4 (over x, core).
Axes of the slice: x: 2, y: 2, z: 4, core: 2. Of those that a mesh axis runs over, the one named last changes fastest.
Arguments:
- frames: bfloat16 [16, 512, 1024], P('dp', 'seq'), may hold values from -6 to 6
- lengths: int32 [16], P('dp'), may hold values from 128 to 512, as said below
- qkv_weight: bfloat16 [1024, 3072], P('dp'), may hold values from -8 to 8, as said below
- out_weight: bfloat16 [1024, 1024], P('dp'), may hold values from -0.75 to 0.75
- cotangent: bfloat16 [16, 512, 1024], P('dp', 'seq'), may hold values from -6 to 6
Outputs:
- result: bfloat16 [16, 512, 1024], P('dp', 'seq')
- frame_grad: bfloat16 [16, 512, 1024], P('dp', 'seq')
- qkv_weight_grad: float32 [1024, 3072], P('dp')
- out_weight_grad: float32 [1024, 1024], P('dp')
The draws below stay inside these ranges and needn't reach their ends.
Inputs may be any that keep to these rules, and one draw needn't show every extreme that they name: `lengths`: valid frames of each recording; in every draw some recording is valid over the whole slab. `qkv_weight`: a projection.
All inputs are finite; a program needn't handle non-finite values.
Results may differ from the reference program's by a relative error of at most 0.023.
The reference program's roundings to bfloat16 on the way count: a program that leaves them out, or rounds other values in their place, can miss the bound.
Values may be sent and summed in bfloat16 or wider, within the bound.
A program may use at most 128 MiB of HBM per device.

```python
import math
import jax
import jax.numpy as jnp
from jax import lax

D = 1024
H = 16
GROUP = 16
LEFT = 64
AHEAD = 4
FR_DEV = 128
SLAB = 512
RECS = 16


def draw_frames(key, part):
    first_key = jax.random.fold_in(jax.random.fold_in(key, 11), 0)
    basic = jax.random.normal(first_key, (RECS, SLAB, D), jnp.float32)
    return jnp.clip(basic, -6.0, 6.0).astype(jnp.bfloat16)


def draw_lengths(key, part):
    first_key, second_key = jax.random.split(jax.random.fold_in(key, 23))
    drawn = jax.random.randint(first_key, (RECS,), SLAB // 4, SLAB + 1)
    chosen = jax.random.randint(second_key, (), 0, RECS)
    return jnp.where(jnp.arange(RECS) == chosen, SLAB, drawn).astype(jnp.int32)


def draw_qkv_weight(key, part):
    first_key = jax.random.fold_in(jax.random.fold_in(key, 37), 0)
    basic = jnp.clip(jax.random.normal(first_key, (D, 3 * D), jnp.float32), -6.0, 6.0) / jnp.sqrt(D * 1.0)
    return basic.astype(jnp.bfloat16)


def steps_of(key, shape, cuts, smallest, high):
    loudness, own = 1.0, jax.random.fold_in(key, 6)
    for dim, shards_of in cuts:
        heights = jnp.exp(jax.random.uniform(jax.random.fold_in(own, dim), (shards_of,), jnp.float32, smallest / len(cuts), high / len(cuts)))
        loudness = loudness * jnp.repeat(heights, shape[dim] // shards_of).reshape([-1 if axis == dim else 1 for axis in range(len(shape))])
    return loudness


def scatter_about(stream_key, shape, scale, most, pieces=(), held_as=jnp.bfloat16):
    entries = jax.random.normal(stream_key, shape, jnp.float32) * scale
    if len(pieces) > 0:
        entries = steps_of(stream_key, shape, pieces, -0.22, 0.18) * entries
    return jnp.clip(entries, min=-most, max=most).astype(held_as)


def setup_inputs(seed: int = 0) -> dict:
    keys = jax.random.split(jax.random.key(seed), 6)
    return {
        "frames": draw_frames(jax.random.fold_in(keys[5], 71), 0),
        "lengths": draw_lengths(jax.random.fold_in(keys[5], 71), 0),
        "qkv_weight": draw_qkv_weight(jax.random.fold_in(keys[5], 71), 0),
        "out_weight": scatter_about(keys[3], (D, D), (D // 16) ** -0.5, 0.75, ((0, 8),)),
        "cotangent": scatter_about(keys[4], (RECS, SLAB, D), 1.0, 6.0, ((0, 8), (1, 4))),
    }


def norm_rows(recording):
    as_float = recording.astype(jnp.float32)
    row_mean = lax.optimization_barrier(jnp.mean(as_float, axis=-1, keepdims=True))
    centred = as_float - row_mean
    variance = lax.optimization_barrier(jnp.mean(centred * centred, axis=-1, keepdims=True))
    inv_std = lax.rsqrt(variance + 1e-05)
    return (centred * inv_std, inv_std)

def window_mask(query_pos, key_pos, rec_length):
    group_start = query_pos // GROUP * GROUP
    inside = (key_pos[None, :] >= 0) & (key_pos[None, :] < SLAB)
    inside = inside & (key_pos[None, :] >= group_start[:, None] - LEFT)
    inside = inside & (key_pos[None, :] < group_start[:, None] + GROUP + AHEAD)
    allowed = (key_pos[None, :] < rec_length) | (query_pos[:, None] >= rec_length)
    return inside & allowed

def attend(queries, key_rows, value_rows, allowed_mask, score_scale):
    scores = jnp.einsum('fhe,khe->hfk', queries.astype(jnp.float32), key_rows.astype(jnp.float32)) * score_scale
    scores = jnp.where(allowed_mask[None], scores, -1e+30)
    row_max = lax.optimization_barrier(jnp.max(scores, axis=-1, keepdims=True))
    shifted = jnp.where(allowed_mask[None], jnp.exp(scores - row_max), 0.0)
    attn_probs = shifted / lax.optimization_barrier(jnp.sum(shifted, axis=-1, keepdims=True))
    probs_half = attn_probs.astype(jnp.bfloat16)
    mixed_rows = jnp.einsum('hfk,khe->fhe', probs_half.astype(jnp.float32), value_rows.astype(jnp.float32))
    return (mixed_rows.astype(jnp.bfloat16), attn_probs, probs_half)

def attend_back(queries, key_rows, value_rows, attn_probs, probs_half, mixed_grad, score_scale):
    value_grad = jnp.einsum('hfk,fhe->khe', probs_half.astype(jnp.float32), mixed_grad.astype(jnp.float32))
    prob_grad = jnp.einsum('fhe,khe->hfk', mixed_grad.astype(jnp.float32), value_rows.astype(jnp.float32))
    score_grad = attn_probs * (prob_grad - lax.optimization_barrier(jnp.sum(attn_probs * prob_grad, axis=-1, keepdims=True))) * score_scale
    score_grad = score_grad.astype(jnp.bfloat16).astype(jnp.float32)
    query_grad = jnp.einsum('hfk,khe->fhe', score_grad, key_rows.astype(jnp.float32))
    key_grad = jnp.einsum('hfk,fhe->khe', score_grad, queries.astype(jnp.float32))
    return (query_grad, key_grad, value_grad)

def reference(frames, lengths, qkv_weight, out_weight, cotangent):
    head_size = D // H
    span_len = FR_DEV + LEFT + AHEAD
    score_scale = 1.0 / math.sqrt(head_size)
    num_blocks = SLAB // FR_DEV

    def one_recording(totals, inputs):
        recording, rec_length, rec_cot = inputs
        centred, inv_std = norm_rows(recording)
        normed = centred.astype(jnp.bfloat16)
        projected_qkv = jnp.dot(normed, qkv_weight, preferred_element_type=jnp.float32).astype(jnp.bfloat16)
        all_queries = projected_qkv[:, :D].reshape(SLAB, H, head_size)
        key_value = jnp.pad(projected_qkv[:, D:], ((LEFT, AHEAD), (0, 0)))
        positions = jnp.arange(SLAB, dtype=jnp.int32)

        def block_inputs(block):
            first = (block * FR_DEV).astype(jnp.int32)
            queries = lax.dynamic_slice_in_dim(all_queries, first, FR_DEV, 0)
            window = lax.dynamic_slice_in_dim(key_value, first, span_len, 0)
            key_rows = window[:, :D].reshape(span_len, H, head_size)
            value_rows = window[:, D:].reshape(span_len, H, head_size)
            query_pos = first + jnp.arange(FR_DEV, dtype=jnp.int32)
            key_pos = first - LEFT + jnp.arange(span_len, dtype=jnp.int32)
            return (queries, key_rows, value_rows, window_mask(query_pos, key_pos, rec_length))

        def forward(block):
            queries, key_rows, value_rows, allowed_mask = block_inputs(block)
            mixed_rows, unused_a, unused_b = attend(queries, key_rows, value_rows, allowed_mask, score_scale)
            return mixed_rows.reshape(FR_DEV, D)
        blocks = jnp.arange(num_blocks, dtype=jnp.int32)
        mixed = lax.map(forward, blocks).reshape(SLAB, D)
        projected = jnp.dot(mixed, out_weight, preferred_element_type=jnp.float32)
        is_valid = (positions < rec_length)[:, None]
        result = jnp.where(is_valid, projected, 0.0).astype(jnp.bfloat16)
        out_grad = jnp.where(is_valid, rec_cot, jnp.zeros_like(rec_cot))
        mixed_grad = jnp.dot(out_grad, out_weight.T, preferred_element_type=jnp.float32).astype(jnp.bfloat16)

        def backward(key_acc, block):
            queries, key_rows, value_rows, allowed_mask = block_inputs(block)
            unused_m, attn_probs, probs_half = attend(queries, key_rows, value_rows, allowed_mask, score_scale)
            first = (block * FR_DEV).astype(jnp.int32)
            grad_rows = lax.dynamic_slice_in_dim(mixed_grad, first, FR_DEV, 0).reshape(FR_DEV, H, head_size)
            query_grad, key_grad, value_grad = attend_back(queries, key_rows, value_rows, attn_probs, probs_half, grad_rows, score_scale)
            piece_grad = jnp.concatenate([key_grad.reshape(span_len, D), value_grad.reshape(span_len, D)], axis=-1)
            current = lax.dynamic_slice_in_dim(key_acc, first, span_len, 0)
            key_acc = lax.dynamic_update_slice_in_dim(key_acc, current + piece_grad, first, 0)
            return (key_acc, query_grad.reshape(FR_DEV, D).astype(jnp.bfloat16))
        key_acc = jnp.zeros((SLAB + LEFT + AHEAD, 2 * D), jnp.float32)
        key_acc, query_blocks = lax.scan(backward, key_acc, blocks)
        qkv_grad = jnp.concatenate([query_blocks.reshape(SLAB, D), key_acc[LEFT:LEFT + SLAB].astype(jnp.bfloat16)], axis=-1)
        qkv_total, out_total = totals
        qkv_total = qkv_total + jnp.dot(normed.T, qkv_grad, preferred_element_type=jnp.float32)
        out_total = out_total + jnp.dot(mixed.T, out_grad, preferred_element_type=jnp.float32)
        norm_grad = jnp.dot(qkv_grad, qkv_weight.T, preferred_element_type=jnp.float32)
        mean_one = lax.optimization_barrier(jnp.mean(norm_grad, axis=-1, keepdims=True))
        mean_two = lax.optimization_barrier(jnp.mean(norm_grad * centred, axis=-1, keepdims=True))
        frame_grad = ((norm_grad - mean_one - centred * mean_two) * inv_std).astype(jnp.bfloat16)
        return ((qkv_total, out_total), (result, frame_grad))
    start_totals = (jnp.zeros((D, 3 * D), jnp.float32), jnp.zeros((D, D), jnp.float32))
    totals, outputs = lax.scan(one_recording, start_totals, (frames, lengths, cotangent))
    return (outputs[0], outputs[1], totals[0], totals[1])
```

```python
import math

import jax
import jax.numpy as jnp
from jax import lax
from jax.sharding import PartitionSpec as P

H = 16
GROUP = 16
LEFT = 64
AHEAD = 4
BLOCK = 128


def norm_rows(frames):
    as_float = frames.astype(jnp.float32)
    row_mean = jnp.mean(as_float, axis=-1, keepdims=True)
    centred = as_float - row_mean
    variance = jnp.mean(centred * centred, axis=-1, keepdims=True)
    inv_std = lax.rsqrt(variance + 1e-05)
    return (centred * inv_std, inv_std)


def window_mask(query_pos, key_pos, lengths, slab_len):
    group_start = query_pos // GROUP * GROUP
    inside = (key_pos[None, :] >= 0) & (key_pos[None, :] < slab_len)
    inside = inside & (key_pos[None, :] >= group_start[:, None] - LEFT)
    inside = inside & (key_pos[None, :] < group_start[:, None] + GROUP + AHEAD)
    allowed = (key_pos[None, None, :] < lengths[:, None, None]) | (
        query_pos[None, :, None] >= lengths[:, None, None]
    )
    return inside[None] & allowed


def attend(queries, key_rows, value_rows, allowed_mask, score_scale):
    scores = (
        jnp.einsum("bfhe,bkhe->bhfk", queries, key_rows, preferred_element_type=jnp.float32)
        * score_scale
    )
    wide_mask = allowed_mask[:, None]
    scores = jnp.where(wide_mask, scores, -1e30)
    row_max = jnp.max(scores, axis=-1, keepdims=True)
    shifted = jnp.where(wide_mask, jnp.exp(scores - row_max), 0.0)
    attn_probs = shifted / jnp.sum(shifted, axis=-1, keepdims=True)
    probs_half = attn_probs.astype(jnp.bfloat16)
    mixed_rows = jnp.einsum(
        "bhfk,bkhe->bfhe", probs_half, value_rows, preferred_element_type=jnp.float32
    )
    return (mixed_rows.astype(jnp.bfloat16), attn_probs, probs_half)


def attend_back(queries, key_rows, value_rows, attn_probs, probs_half, mixed_grad, score_scale):
    value_grad = jnp.einsum(
        "bhfk,bfhe->bkhe", probs_half, mixed_grad, preferred_element_type=jnp.float32
    )
    prob_grad = jnp.einsum(
        "bfhe,bkhe->bhfk", mixed_grad, value_rows, preferred_element_type=jnp.float32
    )
    score_grad = (
        attn_probs
        * (prob_grad - jnp.sum(attn_probs * prob_grad, axis=-1, keepdims=True))
        * score_scale
    )
    score_grad = score_grad.astype(jnp.bfloat16)
    query_grad = jnp.einsum(
        "bhfk,bkhe->bfhe", score_grad, key_rows, preferred_element_type=jnp.float32
    )
    key_grad = jnp.einsum(
        "bhfk,bfhe->bkhe", score_grad, queries, preferred_element_type=jnp.float32
    )
    return (query_grad, key_grad, value_grad)


def per_device(frames, lengths, qkv_weight, out_weight, cotangent):
    records, frame_count, model_width = frames.shape
    head_size = model_width // H
    seq_size = lax.axis_size("seq")
    seq_index = lax.axis_index("seq")
    wide = model_width // seq_size
    heads = wide // head_size
    slab_len = frame_count * seq_size
    row_count = records * slab_len
    blocks = slab_len // BLOCK
    span = BLOCK + LEFT + AHEAD
    score_scale = 1.0 / math.sqrt(head_size)

    shard_rows = qkv_weight.shape[0]
    qkv_mine = lax.dynamic_index_in_dim(
        qkv_weight.reshape(shard_rows, 3, seq_size, wide), seq_index, 2, False
    ).reshape(shard_rows, 3 * wide)
    out_mine = lax.dynamic_slice_in_dim(out_weight, seq_index * wide, wide, 1)
    weights = lax.all_gather(
        jnp.concatenate([qkv_mine, out_mine], axis=1), "dp", axis=0, tiled=True
    )
    both = lax.all_gather(
        jnp.stack([frames, cotangent]), "seq", axis=2, tiled=True
    )
    qkv_cols = weights[:, : 3 * wide]
    out_rows = lax.all_to_all(
        weights[:, 3 * wide :].reshape(seq_size, wide, wide), "seq", 0, 0
    )
    out_rows = jnp.swapaxes(out_rows, 0, 1).reshape(wide, model_width)

    centred, _ = norm_rows(both[0])
    normed = centred.astype(jnp.bfloat16).reshape(row_count, model_width)
    positions = jnp.arange(slab_len, dtype=jnp.int32)
    is_valid = (positions[None, :] < lengths[:, None])[:, :, None]
    out_grad = jnp.where(is_valid, both[1], jnp.zeros_like(both[1])).reshape(row_count, model_width)

    qkv = jnp.dot(normed, qkv_cols, preferred_element_type=jnp.float32).astype(jnp.bfloat16)
    qkv = qkv.reshape(records, slab_len, 3, heads, head_size)
    queries = qkv[:, :, 0].reshape(records * blocks, BLOCK, heads, head_size)

    def windows(value):
        padded = jnp.pad(value, ((0, 0), (LEFT, AHEAD), (0, 0), (0, 0)))
        cut = [padded[:, b * BLOCK : b * BLOCK + span] for b in range(blocks)]
        return jnp.stack(cut, axis=1).reshape(records * blocks, span, heads, head_size)

    key_rows, value_rows = windows(qkv[:, :, 1]), windows(qkv[:, :, 2])
    masks = []
    for b in range(blocks):
        query_pos = b * BLOCK + jnp.arange(BLOCK, dtype=jnp.int32)
        key_pos = b * BLOCK - LEFT + jnp.arange(span, dtype=jnp.int32)
        masks.append(window_mask(query_pos, key_pos, lengths, slab_len))
    allowed_mask = jnp.stack(masks, axis=1).reshape(records * blocks, BLOCK, span)
    mixed, attn_probs, probs_half = attend(
        queries, key_rows, value_rows, allowed_mask, score_scale
    )
    mixed_flat = mixed.reshape(row_count, wide)
    partial = jnp.dot(mixed_flat, out_rows, preferred_element_type=jnp.float32)
    partial = partial.astype(jnp.bfloat16).reshape(records, slab_len, model_width)
    result = lax.psum_scatter(partial, "seq", scatter_dimension=1, tiled=True)
    own_pos = seq_index * frame_count + jnp.arange(frame_count, dtype=jnp.int32)
    own_valid = (own_pos[None, :] < lengths[:, None])[:, :, None]
    result = jnp.where(own_valid, result, jnp.zeros_like(result))

    mixed_grad = lax.dot_general(
        out_grad, out_rows, (((1,), (1,)), ((), ())), preferred_element_type=jnp.float32
    )
    mixed_grad = mixed_grad.astype(jnp.bfloat16).reshape(records * blocks, BLOCK, heads, head_size)
    query_grad, key_grad, value_grad = attend_back(
        queries, key_rows, value_rows, attn_probs, probs_half, mixed_grad, score_scale
    )

    def fold(value):
        value = value.reshape(records, blocks, span, wide)
        total = value[:, :, LEFT : LEFT + BLOCK]
        total = total.at[:, :-1, BLOCK - LEFT :].add(value[:, 1:, :LEFT])
        total = total.at[:, 1:, :AHEAD].add(value[:, :-1, LEFT + BLOCK :])
        return total.reshape(row_count, wide).astype(jnp.bfloat16)

    qkv_grad = jnp.concatenate(
        [query_grad.reshape(row_count, wide).astype(jnp.bfloat16), fold(key_grad), fold(value_grad)],
        axis=1,
    )
    norm_part = lax.dot_general(
        qkv_grad, qkv_cols, (((1,), (1,)), ((), ())), preferred_element_type=jnp.float32
    )
    norm_part = norm_part.astype(jnp.bfloat16).reshape(records, slab_len, model_width)
    norm_grad = lax.psum_scatter(norm_part, "seq", scatter_dimension=1, tiled=True)
    norm_grad = norm_grad.astype(jnp.float32)
    part_out = lax.dot_general(
        mixed_flat, out_grad, (((0,), (0,)), ((), ())), preferred_element_type=jnp.float32
    ).astype(jnp.bfloat16)
    part_out = lax.all_to_all(
        jnp.swapaxes(part_out.reshape(wide, seq_size, wide), 0, 1), "seq", 0, 0
    ).reshape(model_width, wide)
    part_qkv = lax.dot_general(
        normed, qkv_grad, (((0,), (0,)), ((), ())), preferred_element_type=jnp.float32
    ).astype(jnp.bfloat16)
    part = jnp.concatenate([part_qkv, part_out], axis=1)
    part = lax.psum_scatter(part, "dp", scatter_dimension=0, tiled=True)
    full = lax.all_gather(part, "seq", axis=0)
    full = full.reshape(seq_size, shard_rows, 4, wide).astype(jnp.float32)
    full = full.transpose(1, 2, 0, 3).reshape(shard_rows, 4 * model_width)
    qkv_weight_grad = full[:, : 3 * model_width]
    out_weight_grad = full[:, 3 * model_width :]

    centred, inv_std = norm_rows(frames)
    mean_one = jnp.mean(norm_grad, axis=-1, keepdims=True)
    mean_two = jnp.mean(norm_grad * centred, axis=-1, keepdims=True)
    frame_grad = ((norm_grad - mean_one - centred * mean_two) * inv_std).astype(jnp.bfloat16)
    return (result, frame_grad, qkv_weight_grad, out_weight_grad)


def solution(mesh):
    in_specs = (P("dp", "seq", None), P("dp"), P("dp", None), P("dp", None), P("dp", "seq", None))
    out_specs = (P("dp", "seq", None), P("dp", "seq", None), P("dp", None), P("dp", None))
    return jax.shard_map(
        per_device, mesh=mesh, in_specs=in_specs, out_specs=out_specs, check_vma=False
    )
```

```python
import functools
import math

import jax
import jax.numpy as jnp
from jax import lax
from jax.experimental import pallas as pl
from jax.experimental.pallas import tpu as pltpu
from jax.sharding import PartitionSpec as P

H = 16
GROUP = 16
LEFT = 64
AHEAD = 4
BLOCK = 128
PAD = 64
SPAN = BLOCK + 2 * PAD
MESH = pl.DeviceIdType.MESH
BF = jnp.bfloat16
F32 = jnp.float32
VMEM_LIMIT = 60 * 1024 * 1024


def norm_rows(frames):
    as_float = frames.astype(jnp.float32)
    row_mean = jnp.mean(as_float, axis=-1, keepdims=True)
    centred = as_float - row_mean
    variance = jnp.mean(centred * centred, axis=-1, keepdims=True)
    inv_std = lax.rsqrt(variance + 1e-05)
    return (centred * inv_std, inv_std)


def greet(seq_size, dp_size):
    s, j = lax.axis_index("seq"), lax.axis_index("dp")
    barrier = pltpu.get_barrier_semaphore()
    for d in range(1, seq_size):
        pl.semaphore_signal(
            barrier, inc=1, device_id=(j, lax.rem(s + d, seq_size)), device_id_type=MESH
        )
    for d in range(1, dp_size):
        pl.semaphore_signal(
            barrier, inc=1, device_id=(lax.rem(j + d, dp_size), s), device_id_type=MESH
        )
    pl.semaphore_wait(barrier, seq_size + dp_size - 2)


def gather_kernel(
    seq_size, dp_size, fr, ct, wq, wo, fr_all, ct_all, wq_all, wo_all, wo_mine,
    act_send, act_recv, w_send, w_recv, x_send, x_recv, own_sem,
):
    s, j = lax.axis_index("seq"), lax.axis_index("dp")
    frame_count, shard = fr.shape[1], wq.shape[0]
    wide = wo.shape[1]
    outer, core = s // 2, lax.rem(s, 2)
    outers = seq_size // 2
    zed, why = j // 2, lax.rem(j, 2)
    zeds = dp_size // 2
    greet(seq_size, dp_size)

    def act(k, src, dst_all, owner, to, slot, own):
        place = dst_all.at[:, pl.ds(owner * frame_count, frame_count)]
        return pltpu.make_async_remote_copy(
            src_ref=src if own else place, dst_ref=place,
            send_sem=act_send.at[k, slot], recv_sem=act_recv.at[k, slot],
            device_id=(j, to), device_id_type=MESH,
        )

    def weight(k, src, dst_all, owner, to, slot, own):
        place = dst_all.at[pl.ds(owner * shard, shard)]
        return pltpu.make_async_remote_copy(
            src_ref=src if own else place, dst_ref=place,
            send_sem=w_send.at[k, slot], recv_sem=w_recv.at[k, slot],
            device_id=(to, s), device_id_type=MESH,
        )

    acts = ((fr, fr_all), (ct, ct_all))
    ws = ((wo, wo_all), (wq, wq_all))
    across, beside, started = {}, [], []
    for k, (src, dst) in enumerate(ws):
        for d in range(1, zeds):
            c = weight(k, src, dst, j, lax.rem(zed + d, zeds) * 2 + why, d, True)
            c.start()
            across["w", k, d] = c
    for k, (src, dst) in enumerate(acts):
        for d in range(1, outers):
            c = act(k, src, dst, s, lax.rem(outer + d, outers) * 2 + core, d, True)
            c.start()
            across["a", k, d] = c
    for k, (src, dst) in enumerate(ws):
        c = weight(k, src, dst, j, zed * 2 + 1 - why, 0, True)
        c.start()
        beside.append(c)
    for k, (src, dst) in enumerate(acts):
        c = act(k, src, dst, s, outer * 2 + 1 - core, 0, True)
        c.start()
        beside.append(c)
    local = [
        pltpu.make_async_copy(fr, fr_all.at[:, pl.ds(s * frame_count, frame_count)], own_sem.at[0]),
        pltpu.make_async_copy(ct, ct_all.at[:, pl.ds(s * frame_count, frame_count)], own_sem.at[1]),
        pltpu.make_async_copy(wq, wq_all.at[pl.ds(j * shard, shard)], own_sem.at[2]),
        pltpu.make_async_copy(wo, wo_all.at[pl.ds(j * shard, shard)], own_sem.at[3]),
    ]
    for c in local:
        c.start()

    def forward_w(k, dst, d):
        across["w", k, d].wait_recv()
        owner = lax.rem(zed + zeds - d, zeds) * 2 + why
        c = weight(k, None, dst, owner, zed * 2 + 1 - why, zeds + d, False)
        c.start()
        return c

    def forward_a(k, dst, d):
        across["a", k, d].wait_recv()
        owner = lax.rem(outer + outers - d, outers) * 2 + core
        c = act(k, None, dst, owner, outer * 2 + 1 - core, outers + d, False)
        c.start()
        return c

    near_out = [forward_w(0, wo_all, d) for d in range(1, zeds)]
    late = [forward_w(1, wq_all, d) for d in range(1, zeds)]
    late += [forward_a(0, fr_all, d) for d in range(1, outers)]
    late += [forward_a(1, ct_all, d) for d in range(1, outers)]
    local[3].wait()
    for c in [beside[0]] + near_out:
        c.wait_recv()
    swaps = []
    for d in range(1, seq_size):
        to = lax.rem(s + d, seq_size)
        c = pltpu.make_async_remote_copy(
            src_ref=wo_all.at[pl.ds(to * wide, wide)], dst_ref=wo_mine.at[s],
            send_sem=x_send.at[d], recv_sem=x_recv.at[d],
            device_id=(j, to), device_id_type=MESH,
        )
        c.start()
        swaps.append(c)
    last = pltpu.make_async_copy(wo_all.at[pl.ds(s * wide, wide)], wo_mine.at[s], own_sem.at[4])
    last.start()
    for c in beside[1:] + late:
        c.wait_recv()
    for c in swaps:
        c.wait_recv()
    for c in list(across.values()) + beside + near_out + late + swaps:
        c.wait_send()
    for c in local[:3] + [last]:
        c.wait()


def gather(frames, cotangent, wq, wo):
    seq_size, dp_size = lax.axis_size("seq"), lax.axis_size("dp")
    records, frame_count, width = frames.shape
    shard, wide = wo.shape
    anywhere = pl.BlockSpec(memory_space=pl.ANY)
    slab = jax.ShapeDtypeStruct((records, frame_count * seq_size, width), BF)
    dma = pltpu.SemaphoreType.DMA
    return pl.pallas_call(
        functools.partial(gather_kernel, seq_size, dp_size),
        out_shape=(
            slab, slab,
            jax.ShapeDtypeStruct((shard * dp_size, 3 * wide), BF),
            jax.ShapeDtypeStruct((shard * dp_size, wide), BF),
            jax.ShapeDtypeStruct((seq_size, wide, wide), BF),
        ),
        in_specs=[anywhere] * 4,
        out_specs=(anywhere,) * 5,
        scratch_shapes=[
            dma((2, seq_size)), dma((2, seq_size)), dma((2, dp_size)), dma((2, dp_size)),
            dma((seq_size,)), dma((seq_size,)), dma((5,)),
        ],
        compiler_params=pltpu.CompilerParams(collective_id=0, has_side_effects=True),
    )(frames, cotangent, wq, wo)


def dot(a, b, ca=1, cb=0):
    return lax.dot_general(a, b, (((ca,), (cb,)), ((), ())), preferred_element_type=F32)


def core_kernel(
    head_size, lengths, fr, ct, wq, wo, result, norm_part, wq_part, wo_part,
    normed, og, qkv, mgrad, mixed, kv_acc, qkv_grad, wq_acc, wo_acc,
):
    rec = pl.program_id(0)
    slab, width = fr.shape[1:]
    wide = wo.shape[0]
    length = lengths[rec]
    scale = 1.0 / math.sqrt(head_size)
    chunk = min(512, slab)
    pair = min(wide, 128)
    per = pair // head_size
    pad_zero = jnp.zeros((PAD, 3 * wide), BF)
    qkv[pl.ds(0, PAD), :] = pad_zero
    qkv[pl.ds(PAD + slab, PAD), :] = pad_zero
    kv_acc[...] = jnp.zeros_like(kv_acc)

    @pl.when(rec == 0)
    def _():
        wq_acc[...] = jnp.zeros_like(wq_acc)
        wo_acc[...] = jnp.zeros_like(wo_acc)

    @pl.loop(0, slab // BLOCK)
    def _(b):
        rows = pl.ds(pl.multiple_of(b * BLOCK, BLOCK), BLOCK)
        normed[rows, :] = norm_rows(fr[0, rows, :])[0].astype(BF)
        pos = b * BLOCK + lax.broadcasted_iota(jnp.int32, (BLOCK, width), 0)
        og[rows, :] = jnp.where(pos < length, ct[0, rows, :].astype(F32), 0.0).astype(BF)

    @pl.loop(0, slab // chunk)
    def _(b):
        start = pl.multiple_of(b * chunk, chunk)
        rows = pl.ds(start, chunk)
        qkv[pl.ds(PAD + start, chunk), :] = dot(normed[rows, :], wq[...]).astype(BF)
        mgrad[rows, :] = dot(og[rows, :], wo[...], 1, 1).astype(BF)

    @pl.loop(0, slab // BLOCK)
    def _(b):
        start = pl.multiple_of(b * BLOCK, BLOCK)
        rows = pl.ds(start, BLOCK)
        window = pl.ds(start, SPAN)
        shape = (per * BLOCK, SPAN)
        t = start + lax.rem(lax.broadcasted_iota(jnp.int32, shape, 0), BLOCK)
        k = start - PAD + lax.broadcasted_iota(jnp.int32, shape, 1)
        c = t - lax.rem(t, GROUP)
        allowed = (k >= 0) & (k < slab) & (k >= c - LEFT) & (k < c + GROUP + AHEAD)
        allowed = allowed & ((k < length) | (t >= length))
        lane = lax.broadcasted_iota(jnp.int32, (BLOCK, pair), 1) // head_size

        def stack(value):
            if per == 1:
                return value
            value = value.astype(F32)
            return jnp.concatenate(
                [jnp.where(lane == i, value, 0.0) for i in range(per)], axis=0
            ).astype(BF)

        def unstack(value):
            out = value[:BLOCK]
            for i in range(1, per):
                out = jnp.where(lane == i, value[i * BLOCK : (i + 1) * BLOCK], out)
            return out

        for p in range(wide // pair):
            cols = pl.ds(p * pair, pair)
            kcols = pl.ds(wide + p * pair, pair)
            vcols = pl.ds(2 * wide + p * pair, pair)
            q = stack(qkv[pl.ds(PAD + start, BLOCK), cols])
            mg = stack(mgrad[rows, cols])
            keys = qkv[window, kcols]
            values = qkv[window, vcols]
            scores = jnp.where(allowed, dot(q, keys, 1, 1) * scale, -1e30)
            shifted = jnp.exp(scores - jnp.max(scores, axis=-1, keepdims=True))
            shifted = jnp.where(allowed, shifted, 0.0)
            probs = shifted / jnp.sum(shifted, axis=-1, keepdims=True)
            half = probs.astype(BF)
            mixed[rows, cols] = unstack(dot(half, values)).astype(BF)
            pg = dot(mg, values, 1, 1)
            sg = probs * (pg - jnp.sum(probs * pg, axis=-1, keepdims=True)) * scale
            sg = sg.astype(BF)
            qkv_grad[rows, cols] = unstack(dot(sg, keys)).astype(BF)
            kv_acc[window, cols] += dot(sg, q, 0, 0)
            kv_acc[window, kcols] += dot(half, mg, 0, 0)

    @pl.loop(0, slab // chunk)
    def _(b):
        start = pl.multiple_of(b * chunk, chunk)
        rows = pl.ds(start, chunk)
        qkv_grad[rows, pl.ds(wide, 2 * wide)] = kv_acc[pl.ds(PAD + start, chunk), :].astype(BF)
        pos = start + lax.broadcasted_iota(jnp.int32, (chunk, width), 0)
        out = jnp.where(pos < length, dot(mixed[rows, :], wo[...]), 0.0)
        result[0, rows, :] = out.astype(BF)
        norm_part[0, rows, :] = dot(qkv_grad[rows, :], wq[...], 1, 1).astype(BF)
        wq_acc[...] += dot(normed[rows, :], qkv_grad[rows, :], 0, 0)
        wo_acc[...] += dot(mixed[rows, :], og[rows, :], 0, 0)

    @pl.when(rec == pl.num_programs(0) - 1)
    def _():
        wq_part[...] = wq_acc[...].astype(BF)
        wo_part[...] = wo_acc[...].astype(BF)


def core(lengths, fr_all, ct_all, wq_all, wo_rows):
    records, slab, width = fr_all.shape
    wide = wo_rows.shape[0]
    per_rec = pl.BlockSpec((1, slab, width), lambda r: (r, 0, 0))
    wq_spec = pl.BlockSpec((width, 3 * wide), lambda r: (0, 0))
    wo_spec = pl.BlockSpec((wide, width), lambda r: (0, 0))
    rows = jax.ShapeDtypeStruct((records, slab, width), BF)
    return pl.pallas_call(
        functools.partial(core_kernel, width // H),
        grid=(records,),
        out_shape=(
            rows, rows,
            jax.ShapeDtypeStruct((width, 3 * wide), BF),
            jax.ShapeDtypeStruct((wide, width), BF),
        ),
        in_specs=[pl.BlockSpec(memory_space=pltpu.SMEM), per_rec, per_rec, wq_spec, wo_spec],
        out_specs=(per_rec, per_rec, wq_spec, wo_spec),
        scratch_shapes=[
            pltpu.VMEM((slab, width), BF),
            pltpu.VMEM((slab, width), BF),
            pltpu.VMEM((slab + 2 * PAD, 3 * wide), BF),
            pltpu.VMEM((slab, wide), BF),
            pltpu.VMEM((slab, wide), BF),
            pltpu.VMEM((slab + 2 * PAD, 2 * wide), F32),
            pltpu.VMEM((slab, 3 * wide), BF),
            pltpu.VMEM((width, 3 * wide), F32),
            pltpu.VMEM((wide, width), F32),
        ],
        compiler_params=pltpu.CompilerParams(vmem_limit_bytes=VMEM_LIMIT),
    )(lengths, fr_all, ct_all, wq_all, wo_rows)


def per_device(frames, lengths, qkv_weight, out_weight, cotangent):
    records, frame_count, model_width = frames.shape
    seq_size = lax.axis_size("seq")
    seq_index = lax.axis_index("seq")
    wide = model_width // seq_size
    shard_rows = qkv_weight.shape[0]
    qkv_mine = lax.dynamic_index_in_dim(
        qkv_weight.reshape(shard_rows, 3, seq_size, wide), seq_index, 2, False
    ).reshape(shard_rows, 3 * wide)
    out_mine = lax.dynamic_slice_in_dim(out_weight, seq_index * wide, wide, 1)
    fr_all, ct_all, wq_all, _, wo_mine = gather(frames, cotangent, qkv_mine, out_mine)
    wo_rows = jnp.swapaxes(wo_mine, 0, 1).reshape(wide, model_width)
    partial, norm_part, part_qkv, part_out = core(lengths, fr_all, ct_all, wq_all, wo_rows)
    return finish(frames, partial, norm_part, part_qkv, part_out, shard_rows)


def finish(frames, partial, norm_part, part_qkv, part_out, shard_rows):
    model_width = frames.shape[-1]
    seq_size = lax.axis_size("seq")
    wide = model_width // seq_size
    result = lax.psum_scatter(partial, "seq", scatter_dimension=1, tiled=True)
    norm_grad = lax.psum_scatter(norm_part, "seq", scatter_dimension=1, tiled=True)
    norm_grad = norm_grad.astype(F32)
    part_out = lax.all_to_all(
        jnp.swapaxes(part_out.reshape(wide, seq_size, wide), 0, 1), "seq", 0, 0
    ).reshape(model_width, wide)
    part = jnp.concatenate([part_qkv, part_out], axis=1)
    part = lax.psum_scatter(part, "dp", scatter_dimension=0, tiled=True)
    full = lax.all_gather(part, "seq", axis=0)
    full = full.reshape(seq_size, shard_rows, 4, wide).astype(F32)
    full = full.transpose(1, 2, 0, 3).reshape(shard_rows, 4 * model_width)
    qkv_weight_grad = full[:, : 3 * model_width]
    out_weight_grad = full[:, 3 * model_width :]
    centred, inv_std = norm_rows(frames)
    mean_one = jnp.mean(norm_grad, axis=-1, keepdims=True)
    mean_two = jnp.mean(norm_grad * centred, axis=-1, keepdims=True)
    frame_grad = ((norm_grad - mean_one - centred * mean_two) * inv_std).astype(BF)
    return (result, frame_grad, qkv_weight_grad, out_weight_grad)


def solution(mesh):
    in_specs = (P("dp", "seq", None), P("dp"), P("dp", None), P("dp", None), P("dp", "seq", None))
    out_specs = (P("dp", "seq", None), P("dp", "seq", None), P("dp", None), P("dp", None))
    return jax.shard_map(
        per_device, mesh=mesh, in_specs=in_specs, out_specs=out_specs, check_vma=False
    )
```

```python
import functools
import math

import jax
import jax.numpy as jnp
from jax import lax
from jax.experimental import pallas as pl
from jax.experimental.pallas import tpu as pltpu
from jax.sharding import PartitionSpec as P

H = 16
GROUP = 16
LEFT = 64
AHEAD = 4
BLOCK = 128
PAD = 64
SPAN = BLOCK + 2 * PAD
MESH = pl.DeviceIdType.MESH
BF = jnp.bfloat16
F32 = jnp.float32
VMEM_LIMIT = 60 * 1024 * 1024


def norm_rows(frames):
    as_float = frames.astype(jnp.float32)
    row_mean = jnp.mean(as_float, axis=-1, keepdims=True)
    centred = as_float - row_mean
    variance = jnp.mean(centred * centred, axis=-1, keepdims=True)
    inv_std = lax.rsqrt(variance + 1e-05)
    return (centred * inv_std, inv_std)


def greet(seq_size, dp_size):
    s, j = lax.axis_index("seq"), lax.axis_index("dp")
    barrier = pltpu.get_barrier_semaphore()
    for d in range(1, seq_size):
        pl.semaphore_signal(
            barrier, inc=1, device_id=(j, lax.rem(s + d, seq_size)), device_id_type=MESH
        )
    for d in range(1, dp_size):
        pl.semaphore_signal(
            barrier, inc=1, device_id=(lax.rem(j + d, dp_size), s), device_id_type=MESH
        )
    pl.semaphore_wait(barrier, seq_size + dp_size - 2)


def gather_kernel(
    seq_size, dp_size, fr, ct, wq, wo, fr_all, ct_all, wq_all, wo_all, wo_mine,
    act_send, act_recv, w_send, w_recv, x_send, x_recv, own_sem,
):
    s, j = lax.axis_index("seq"), lax.axis_index("dp")
    frame_count, shard = fr.shape[1], wq.shape[0]
    wide = wo.shape[1]
    outer, core = s // 2, lax.rem(s, 2)
    outers = seq_size // 2
    zed, why = j // 2, lax.rem(j, 2)
    zeds = dp_size // 2
    greet(seq_size, dp_size)

    def act(k, src, dst_all, owner, to, slot, own):
        place = dst_all.at[:, pl.ds(owner * frame_count, frame_count)]
        return pltpu.make_async_remote_copy(
            src_ref=src if own else place, dst_ref=place,
            send_sem=act_send.at[k, slot], recv_sem=act_recv.at[k, slot],
            device_id=(j, to), device_id_type=MESH,
        )

    def weight(k, src, dst_all, owner, to, slot, own):
        place = dst_all.at[pl.ds(owner * shard, shard)]
        return pltpu.make_async_remote_copy(
            src_ref=src if own else place, dst_ref=place,
            send_sem=w_send.at[k, slot], recv_sem=w_recv.at[k, slot],
            device_id=(to, s), device_id_type=MESH,
        )

    acts = ((fr, fr_all), (ct, ct_all))
    ws = ((wo, wo_all), (wq, wq_all))
    across, beside, started = {}, [], []
    for k, (src, dst) in enumerate(ws):
        for d in range(1, zeds):
            c = weight(k, src, dst, j, lax.rem(zed + d, zeds) * 2 + why, d, True)
            c.start()
            across["w", k, d] = c
    for k, (src, dst) in enumerate(acts):
        for d in range(1, outers):
            c = act(k, src, dst, s, lax.rem(outer + d, outers) * 2 + core, d, True)
            c.start()
            across["a", k, d] = c
    for k, (src, dst) in enumerate(ws):
        c = weight(k, src, dst, j, zed * 2 + 1 - why, 0, True)
        c.start()
        beside.append(c)
    for k, (src, dst) in enumerate(acts):
        c = act(k, src, dst, s, outer * 2 + 1 - core, 0, True)
        c.start()
        beside.append(c)
    local = [
        pltpu.make_async_copy(fr, fr_all.at[:, pl.ds(s * frame_count, frame_count)], own_sem.at[0]),
        pltpu.make_async_copy(ct, ct_all.at[:, pl.ds(s * frame_count, frame_count)], own_sem.at[1]),
        pltpu.make_async_copy(wq, wq_all.at[pl.ds(j * shard, shard)], own_sem.at[2]),
        pltpu.make_async_copy(wo, wo_all.at[pl.ds(j * shard, shard)], own_sem.at[3]),
    ]
    for c in local:
        c.start()

    def forward_w(k, dst, d):
        across["w", k, d].wait_recv()
        owner = lax.rem(zed + zeds - d, zeds) * 2 + why
        c = weight(k, None, dst, owner, zed * 2 + 1 - why, zeds + d, False)
        c.start()
        return c

    def forward_a(k, dst, d):
        across["a", k, d].wait_recv()
        owner = lax.rem(outer + outers - d, outers) * 2 + core
        c = act(k, None, dst, owner, outer * 2 + 1 - core, outers + d, False)
        c.start()
        return c

    near_out = [forward_w(0, wo_all, d) for d in range(1, zeds)]
    late = [forward_w(1, wq_all, d) for d in range(1, zeds)]
    late += [forward_a(0, fr_all, d) for d in range(1, outers)]
    late += [forward_a(1, ct_all, d) for d in range(1, outers)]
    local[3].wait()
    for c in [beside[0]] + near_out:
        c.wait_recv()
    swaps = []
    for d in range(1, seq_size):
        to = lax.rem(s + d, seq_size)
        c = pltpu.make_async_remote_copy(
            src_ref=wo_all.at[pl.ds(to * wide, wide)], dst_ref=wo_mine.at[s],
            send_sem=x_send.at[d], recv_sem=x_recv.at[d],
            device_id=(j, to), device_id_type=MESH,
        )
        c.start()
        swaps.append(c)
    last = pltpu.make_async_copy(wo_all.at[pl.ds(s * wide, wide)], wo_mine.at[s], own_sem.at[4])
    last.start()
    for c in beside[1:] + late:
        c.wait_recv()
    for c in swaps:
        c.wait_recv()
    for c in list(across.values()) + beside + near_out + late + swaps:
        c.wait_send()
    for c in local[:3] + [last]:
        c.wait()


def gather(frames, cotangent, wq, wo):
    seq_size, dp_size = lax.axis_size("seq"), lax.axis_size("dp")
    records, frame_count, width = frames.shape
    shard, wide = wo.shape
    anywhere = pl.BlockSpec(memory_space=pl.ANY)
    slab = jax.ShapeDtypeStruct((records, frame_count * seq_size, width), BF)
    dma = pltpu.SemaphoreType.DMA
    return pl.pallas_call(
        functools.partial(gather_kernel, seq_size, dp_size),
        out_shape=(
            slab, slab,
            jax.ShapeDtypeStruct((shard * dp_size, 3 * wide), BF),
            jax.ShapeDtypeStruct((shard * dp_size, wide), BF),
            jax.ShapeDtypeStruct((seq_size, wide, wide), BF),
        ),
        in_specs=[anywhere] * 4,
        out_specs=(anywhere,) * 5,
        scratch_shapes=[
            dma((2, seq_size)), dma((2, seq_size)), dma((2, dp_size)), dma((2, dp_size)),
            dma((seq_size,)), dma((seq_size,)), dma((5,)),
        ],
        compiler_params=pltpu.CompilerParams(collective_id=0, has_side_effects=True),
    )(frames, cotangent, wq, wo)


def dot(a, b, ca=1, cb=0):
    return lax.dot_general(a, b, (((ca,), (cb,)), ((), ())), preferred_element_type=F32)


def core_kernel(
    head_size, lengths, fr, ct, wq, wo, result, norm_part, wq_part, wo_part,
    normed, og, qkv, mgrad, mixed, kv_acc, qkv_grad, wq_acc, wo_acc,
):
    rec = pl.program_id(0)
    slab, width = fr.shape[1:]
    wide = wo.shape[0]
    length = lengths[rec]
    scale = 1.0 / math.sqrt(head_size)
    chunk = min(512, slab)
    pair = min(wide, 128)
    per = pair // head_size
    pad_zero = jnp.zeros((PAD, 3 * wide), BF)
    qkv[pl.ds(0, PAD), :] = pad_zero
    qkv[pl.ds(PAD + slab, PAD), :] = pad_zero
    kv_acc[...] = jnp.zeros_like(kv_acc)

    @pl.when(rec == 0)
    def _():
        wq_acc[...] = jnp.zeros_like(wq_acc)
        wo_acc[...] = jnp.zeros_like(wo_acc)

    @pl.loop(0, slab // BLOCK)
    def _(b):
        rows = pl.ds(pl.multiple_of(b * BLOCK, BLOCK), BLOCK)
        normed[rows, :] = norm_rows(fr[0, rows, :])[0].astype(BF)
        pos = b * BLOCK + lax.broadcasted_iota(jnp.int32, (BLOCK, width), 0)
        og[rows, :] = jnp.where(pos < length, ct[0, rows, :].astype(F32), 0.0).astype(BF)

    @pl.loop(0, slab // chunk)
    def _(b):
        start = pl.multiple_of(b * chunk, chunk)
        rows = pl.ds(start, chunk)
        qkv[pl.ds(PAD + start, chunk), :] = dot(normed[rows, :], wq[...]).astype(BF)
        mgrad[rows, :] = dot(og[rows, :], wo[...], 1, 1).astype(BF)

    @pl.loop(0, slab // BLOCK)
    def _(b):
        start = pl.multiple_of(b * BLOCK, BLOCK)
        rows = pl.ds(start, BLOCK)
        window = pl.ds(start, SPAN)
        shape = (per * BLOCK, SPAN)
        t = start + lax.rem(lax.broadcasted_iota(jnp.int32, shape, 0), BLOCK)
        k = start - PAD + lax.broadcasted_iota(jnp.int32, shape, 1)
        c = t - lax.rem(t, GROUP)
        allowed = (k >= 0) & (k < slab) & (k >= c - LEFT) & (k < c + GROUP + AHEAD)
        allowed = allowed & ((k < length) | (t >= length))
        lane = lax.broadcasted_iota(jnp.int32, (BLOCK, pair), 1) // head_size

        def stack(value):
            if per == 1:
                return value
            value = value.astype(F32)
            return jnp.concatenate(
                [jnp.where(lane == i, value, 0.0) for i in range(per)], axis=0
            ).astype(BF)

        def unstack(value):
            out = value[:BLOCK]
            for i in range(1, per):
                out = jnp.where(lane == i, value[i * BLOCK : (i + 1) * BLOCK], out)
            return out

        for p in range(wide // pair):
            cols = pl.ds(p * pair, pair)
            kcols = pl.ds(wide + p * pair, pair)
            vcols = pl.ds(2 * wide + p * pair, pair)
            q = stack(qkv[pl.ds(PAD + start, BLOCK), cols])
            mg = stack(mgrad[rows, cols])
            keys = qkv[window, kcols]
            values = qkv[window, vcols]
            scores = jnp.where(allowed, dot(q, keys, 1, 1) * scale, -1e30)
            shifted = jnp.exp(scores - jnp.max(scores, axis=-1, keepdims=True))
            shifted = jnp.where(allowed, shifted, 0.0)
            probs = shifted / jnp.sum(shifted, axis=-1, keepdims=True)
            half = probs.astype(BF)
            mixed[rows, cols] = unstack(dot(half, values)).astype(BF)
            pg = dot(mg, values, 1, 1)
            sg = probs * (pg - jnp.sum(probs * pg, axis=-1, keepdims=True)) * scale
            sg = sg.astype(BF)
            qkv_grad[rows, cols] = unstack(dot(sg, keys)).astype(BF)
            kv_acc[window, cols] += dot(sg, q, 0, 0)
            kv_acc[window, kcols] += dot(half, mg, 0, 0)

    @pl.loop(0, slab // chunk)
    def _(b):
        start = pl.multiple_of(b * chunk, chunk)
        rows = pl.ds(start, chunk)
        qkv_grad[rows, pl.ds(wide, 2 * wide)] = kv_acc[pl.ds(PAD + start, chunk), :].astype(BF)
        pos = start + lax.broadcasted_iota(jnp.int32, (chunk, width), 0)
        out = jnp.where(pos < length, dot(mixed[rows, :], wo[...]), 0.0)
        result[0, rows, :] = out.astype(BF)
        norm_part[0, rows, :] = dot(qkv_grad[rows, :], wq[...], 1, 1).astype(BF)
        wq_acc[...] += dot(normed[rows, :], qkv_grad[rows, :], 0, 0)
        wo_acc[...] += dot(mixed[rows, :], og[rows, :], 0, 0)

    @pl.when(rec == pl.num_programs(0) - 1)
    def _():
        wq_part[...] = wq_acc[...].astype(BF)
        for p in range(width // wide):
            wo_part[p] = wo_acc[:, p * wide : (p + 1) * wide].astype(BF)


def core(lengths, fr_all, ct_all, wq_all, wo_rows):
    records, slab, width = fr_all.shape
    wide = wo_rows.shape[0]
    per_rec = pl.BlockSpec((1, slab, width), lambda r: (r, 0, 0))
    wq_spec = pl.BlockSpec((width, 3 * wide), lambda r: (0, 0))
    wo_spec = pl.BlockSpec((wide, width), lambda r: (0, 0))
    rows = jax.ShapeDtypeStruct((records, slab, width), BF)
    return pl.pallas_call(
        functools.partial(core_kernel, width // H),
        grid=(records,),
        out_shape=(
            rows, rows,
            jax.ShapeDtypeStruct((width, 3 * wide), BF),
            jax.ShapeDtypeStruct((width // wide, wide, wide), BF),
        ),
        in_specs=[pl.BlockSpec(memory_space=pltpu.SMEM), per_rec, per_rec, wq_spec, wo_spec],
        out_specs=(
            per_rec, per_rec, wq_spec,
            pl.BlockSpec((width // wide, wide, wide), lambda r: (0, 0, 0)),
        ),
        scratch_shapes=[
            pltpu.VMEM((slab, width), BF),
            pltpu.VMEM((slab, width), BF),
            pltpu.VMEM((slab + 2 * PAD, 3 * wide), BF),
            pltpu.VMEM((slab, wide), BF),
            pltpu.VMEM((slab, wide), BF),
            pltpu.VMEM((slab + 2 * PAD, 2 * wide), F32),
            pltpu.VMEM((slab, 3 * wide), BF),
            pltpu.VMEM((width, 3 * wide), F32),
            pltpu.VMEM((wide, width), F32),
        ],
        compiler_params=pltpu.CompilerParams(vmem_limit_bytes=VMEM_LIMIT),
    )(lengths, fr_all, ct_all, wq_all, wo_rows)


def per_device(frames, lengths, qkv_weight, out_weight, cotangent):
    records, frame_count, model_width = frames.shape
    seq_size = lax.axis_size("seq")
    seq_index = lax.axis_index("seq")
    wide = model_width // seq_size
    shard_rows = qkv_weight.shape[0]
    qkv_mine = lax.dynamic_index_in_dim(
        qkv_weight.reshape(shard_rows, 3, seq_size, wide), seq_index, 2, False
    ).reshape(shard_rows, 3 * wide)
    out_mine = lax.dynamic_slice_in_dim(out_weight, seq_index * wide, wide, 1)
    fr_all, ct_all, wq_all, _, wo_mine = gather(frames, cotangent, qkv_mine, out_mine)
    wo_rows = jnp.swapaxes(wo_mine, 0, 1).reshape(wide, model_width)
    partial, norm_part, part_qkv, part_out = core(lengths, fr_all, ct_all, wq_all, wo_rows)
    return reduce_all(frames, partial, norm_part, part_qkv, part_out, shard_rows)


def reduce_kernel(
    seq_size, dp_size, fr, res_part, norm_part, wq_part, wo_part,
    result, frame_grad, qkv_out, out_out,
    wo_cols, near_r, far_r, near_n, far_n, near_q, far_q, near_o, far_o,
    mine_q, mine_o, got_q, got_o, send_sem, recv_sem, own_sem,
):
    s, j = lax.axis_index("seq"), lax.axis_index("dp")
    records, frame_count, width = fr.shape
    wide = wo_part.shape[1]
    shard = qkv_out.shape[0]
    greet(seq_size, dp_size)
    every = []

    def start(src, dst, to):
        n = len(every)
        c = pltpu.make_async_remote_copy(
            src_ref=src, dst_ref=dst, send_sem=send_sem.at[n], recv_sem=recv_sem.at[n],
            device_id=to, device_id_type=MESH,
        )
        c.start()
        every.append(c)
        return c

    class Hop:
        def __init__(self, block, near, far, me, size, device):
            self.block, self.near, self.far = block, near, far
            self.hi, self.lo, self.his = me // 2, lax.rem(me, 2), size // 2
            self.device = device

        def first(self):
            self.coming = {}
            for d in list(range(1, self.his)) + [0]:
                owner = lax.rem(self.hi + d, self.his) * 2 + 1 - self.lo
                self.coming[d] = start(
                    self.block(owner), self.near.at[d], self.device(self.hi * 2 + 1 - self.lo)
                )

        def second(self):
            self.late = []
            for d in range(1, self.his):
                self.coming[d].wait_recv()
                owner = lax.rem(self.hi + d, self.his) * 2 + self.lo
                own = self.block(owner)
                each_chunk(self.near.at[d], lambda at: put(
                    self.near.at[d], at, self.near.at[d][at].astype(F32) + own[at].astype(F32)
                ))
                self.late.append(start(self.near.at[d], self.far.at[d], self.device(owner)))

        def wait(self):
            self.coming[0].wait_recv()
            for c in self.late:
                c.wait_recv()
            self.own = self.block(self.hi * 2 + self.lo)

        def total(self, at):
            value = self.near.at[0][at].astype(F32) + self.own[at].astype(F32)
            for d in range(1, self.his):
                value = value + self.far.at[d][at].astype(F32)
            return value

    def put(ref, at, value):
        ref[at] = value.astype(ref.dtype)

    def each_chunk(ref, body):
        if len(ref.shape) == 3:
            for r in range(ref.shape[0]):
                @pl.loop(0, ref.shape[1] // 32)
                def _(b):
                    body((r, pl.ds(pl.multiple_of(b * 32, 32), 32)))
        else:
            @pl.loop(0, ref.shape[0] // 32)
            def _(b):
                body((pl.ds(pl.multiple_of(b * 32, 32), 32),))

    on_dp = lambda i: (i, s)
    on_seq = lambda i: (j, i)
    frame_block = lambda ref: lambda i: ref.at[:, pl.ds(i * frame_count, frame_count)]
    row_block = lambda ref: lambda i: ref.at[pl.ds(i * shard, shard)]
    hop_q = Hop(row_block(wq_part), near_q, far_q, j, dp_size, on_dp)
    hop_o = Hop(row_block(wo_cols), near_o, far_o, j, dp_size, on_dp)
    hop_n = Hop(frame_block(norm_part), near_n, far_n, s, seq_size, on_seq)
    hop_r = Hop(frame_block(res_part), near_r, far_r, s, seq_size, on_seq)

    swaps = []
    hop_q.first()
    for d in range(1, seq_size):
        to = lax.rem(s + d, seq_size)
        swaps.append(start(wo_part.at[to], wo_cols.at[pl.ds(s * wide, wide)], on_seq(to)))
    own = pltpu.make_async_copy(wo_part.at[s], wo_cols.at[pl.ds(s * wide, wide)], own_sem)
    own.start()
    hop_n.first()
    hop_r.first()
    own.wait()
    for c in swaps:
        c.wait_recv()
    hop_o.first()
    hop_n.second()
    hop_q.second()
    hop_o.second()
    hop_r.second()

    hop_n.wait()

    def normalise(at):
        centred, inv_std = norm_rows(fr[at])
        grad = hop_n.total(at)
        one = jnp.mean(grad, axis=-1, keepdims=True)
        two = jnp.mean(grad * centred, axis=-1, keepdims=True)
        frame_grad[at] = ((grad - one - centred * two) * inv_std).astype(BF)

    each_chunk(fr, normalise)

    hop_q.wait()
    each_chunk(mine_q, lambda at: put(mine_q, at, hop_q.total(at)))
    hop_o.wait()
    each_chunk(mine_o, lambda at: put(mine_o, at, hop_o.total(at)))
    arrivals = {}
    for d in range(1, seq_size):
        to = lax.rem(s + d, seq_size)
        arrivals[d] = (
            start(mine_q, got_q.at[s], on_seq(to)), start(mine_o, got_o.at[s], on_seq(to))
        )

    hop_r.wait()
    each_chunk(result, lambda at: put(result, at, hop_r.total(at)))

    local = [
        pltpu.make_async_copy(mine_q, got_q.at[s], own_sem),
        pltpu.make_async_copy(mine_o, got_o.at[s], own_sem),
    ]
    for c in local:
        c.start()
        c.wait()
    for pair in arrivals.values():
        for c in pair:
            c.wait_recv()
    for p in range(seq_size):
        for k in range(3):
            qkv_out[:, k * width + p * wide : k * width + (p + 1) * wide] = got_q[
                p, :, k * wide : (k + 1) * wide
            ].astype(F32)
        out_out[:, p * wide : (p + 1) * wide] = got_o[p].astype(F32)
    for c in every:
        c.wait_send()


def reduce_all(frames, partial, norm_part, part_qkv, part_out, shard):
    records, frame_count, width = frames.shape
    seq_size, dp_size = lax.axis_size("seq"), lax.axis_size("dp")
    wide = width // seq_size
    vmem = pl.BlockSpec(memory_space=pltpu.VMEM)
    outers, zeds = seq_size // 2, dp_size // 2
    act = pltpu.VMEM((outers, records, frame_count, width), BF)
    wq = pltpu.VMEM((zeds, shard, 3 * wide), BF)
    wo = pltpu.VMEM((zeds, shard, wide), BF)
    copies = 4 * (seq_size + dp_size) + 3 * seq_size
    return pl.pallas_call(
        functools.partial(reduce_kernel, seq_size, dp_size),
        out_shape=(
            jax.ShapeDtypeStruct(frames.shape, BF),
            jax.ShapeDtypeStruct(frames.shape, BF),
            jax.ShapeDtypeStruct((shard, 3 * width), F32),
            jax.ShapeDtypeStruct((shard, width), F32),
        ),
        in_specs=[vmem] * 5,
        out_specs=(vmem,) * 4,
        scratch_shapes=[
            pltpu.VMEM((width, wide), BF),
            act, act, act, act, wq, wq, wo, wo,
            pltpu.VMEM((shard, 3 * wide), BF),
            pltpu.VMEM((shard, wide), BF),
            pltpu.VMEM((seq_size, shard, 3 * wide), BF),
            pltpu.VMEM((seq_size, shard, wide), BF),
            pltpu.SemaphoreType.DMA((copies,)),
            pltpu.SemaphoreType.DMA((copies,)),
            pltpu.SemaphoreType.DMA,
        ],
        compiler_params=pltpu.CompilerParams(
            collective_id=1, has_side_effects=True, vmem_limit_bytes=VMEM_LIMIT
        ),
    )(frames, partial, norm_part, part_qkv, part_out)


def solution(mesh):
    in_specs = (P("dp", "seq", None), P("dp"), P("dp", None), P("dp", None), P("dp", "seq", None))
    out_specs = (P("dp", "seq", None), P("dp", "seq", None), P("dp", None), P("dp", None))
    return jax.shard_map(
        per_device, mesh=mesh, in_specs=in_specs, out_specs=out_specs, check_vma=False
    )
```

```python
import functools
import math

import jax
import jax.numpy as jnp
from jax import lax
from jax.experimental import pallas as pl
from jax.experimental.pallas import tpu as pltpu
from jax.sharding import PartitionSpec as P

H = 16
GROUP = 16
LEFT = 64
AHEAD = 4
BLOCK = 128
PAD = 64
SPAN = BLOCK + 2 * PAD
MESH = pl.DeviceIdType.MESH
BF = jnp.bfloat16
F32 = jnp.float32
VMEM_LIMIT = 60 * 1024 * 1024


def norm_rows(frames):
    as_float = frames.astype(jnp.float32)
    row_mean = jnp.mean(as_float, axis=-1, keepdims=True)
    centred = as_float - row_mean
    variance = jnp.mean(centred * centred, axis=-1, keepdims=True)
    inv_std = lax.rsqrt(variance + 1e-05)
    return (centred * inv_std, inv_std)


def greet(seq_size, dp_size):
    s, j = lax.axis_index("seq"), lax.axis_index("dp")
    barrier = pltpu.get_barrier_semaphore()
    for d in range(1, seq_size):
        pl.semaphore_signal(
            barrier, inc=1, device_id=(j, lax.rem(s + d, seq_size)), device_id_type=MESH
        )
    for d in range(1, dp_size):
        pl.semaphore_signal(
            barrier, inc=1, device_id=(lax.rem(j + d, dp_size), s), device_id_type=MESH
        )
    pl.semaphore_wait(barrier, seq_size + dp_size - 2)


def gather_kernel(
    seq_size, dp_size, fr, ct, wq, wo, fr_all, ct_all, wq_all, wo_all, wo_mine,
    act_send, act_recv, w_send, w_recv, x_send, x_recv, own_sem,
):
    s, j = lax.axis_index("seq"), lax.axis_index("dp")
    frame_count, shard = fr.shape[1], wq.shape[0]
    wide = wo.shape[1]
    outer, core = s // 2, lax.rem(s, 2)
    outers = seq_size // 2
    zed, why = j // 2, lax.rem(j, 2)
    zeds = dp_size // 2
    greet(seq_size, dp_size)

    def act(k, src, dst_all, owner, to, slot, own):
        place = dst_all.at[:, pl.ds(owner * frame_count, frame_count)]
        return pltpu.make_async_remote_copy(
            src_ref=src if own else place, dst_ref=place,
            send_sem=act_send.at[k, slot], recv_sem=act_recv.at[k, slot],
            device_id=(j, to), device_id_type=MESH,
        )

    def weight(k, src, dst_all, owner, to, slot, own):
        first, count = ((0, shard), (0, shard // 2), (shard // 2, shard // 2))[k]
        place = dst_all.at[pl.ds(owner * shard + first, count)]
        return pltpu.make_async_remote_copy(
            src_ref=src.at[pl.ds(first, count)] if own else place, dst_ref=place,
            send_sem=w_send.at[k, slot], recv_sem=w_recv.at[k, slot],
            device_id=(to, s), device_id_type=MESH,
        )

    acts = ((fr, fr_all), (ct, ct_all))
    ws = ((wo, wo_all), (wq, wq_all), (wq, wq_all))
    across, beside, started = {}, [], []
    for k, (src, dst) in enumerate(ws):
        for d in range(1, zeds):
            c = weight(k, src, dst, j, lax.rem(zed + d, zeds) * 2 + why, d, True)
            c.start()
            across["w", k, d] = c
    for k, (src, dst) in enumerate(acts):
        for d in range(1, outers):
            c = act(k, src, dst, s, lax.rem(outer + d, outers) * 2 + core, d, True)
            c.start()
            across["a", k, d] = c
    for k, (src, dst) in enumerate(ws):
        c = weight(k, src, dst, j, zed * 2 + 1 - why, 0, True)
        c.start()
        beside.append(c)
    for k, (src, dst) in enumerate(acts):
        c = act(k, src, dst, s, outer * 2 + 1 - core, 0, True)
        c.start()
        beside.append(c)
    local = [
        pltpu.make_async_copy(fr, fr_all.at[:, pl.ds(s * frame_count, frame_count)], own_sem.at[0]),
        pltpu.make_async_copy(ct, ct_all.at[:, pl.ds(s * frame_count, frame_count)], own_sem.at[1]),
        pltpu.make_async_copy(wq, wq_all.at[pl.ds(j * shard, shard)], own_sem.at[2]),
        pltpu.make_async_copy(wo, wo_all.at[pl.ds(j * shard, shard)], own_sem.at[3]),
    ]
    for c in local:
        c.start()

    def forward_w(k, dst, d):
        across["w", k, d].wait_recv()
        owner = lax.rem(zed + zeds - d, zeds) * 2 + why
        c = weight(k, None, dst, owner, zed * 2 + 1 - why, zeds + d, False)
        c.start()
        return c

    def forward_a(k, dst, d):
        across["a", k, d].wait_recv()
        owner = lax.rem(outer + outers - d, outers) * 2 + core
        c = act(k, None, dst, owner, outer * 2 + 1 - core, outers + d, False)
        c.start()
        return c

    near_out = [forward_w(0, wo_all, d) for d in range(1, zeds)]
    late = [forward_w(k, wq_all, d) for k in (1, 2) for d in range(1, zeds)]
    late += [forward_a(0, fr_all, d) for d in range(1, outers)]
    late += [forward_a(1, ct_all, d) for d in range(1, outers)]
    local[3].wait()
    for c in [beside[0]] + near_out:
        c.wait_recv()
    swaps = []
    for d in range(1, seq_size):
        to = lax.rem(s + d, seq_size)
        c = pltpu.make_async_remote_copy(
            src_ref=wo_all.at[pl.ds(to * wide, wide)], dst_ref=wo_mine.at[s],
            send_sem=x_send.at[d], recv_sem=x_recv.at[d],
            device_id=(j, to), device_id_type=MESH,
        )
        c.start()
        swaps.append(c)
    last = pltpu.make_async_copy(wo_all.at[pl.ds(s * wide, wide)], wo_mine.at[s], own_sem.at[4])
    last.start()
    for c in beside[1:] + late:
        c.wait_recv()
    for c in swaps:
        c.wait_recv()
    for c in list(across.values()) + beside + near_out + late + swaps:
        c.wait_send()
    for c in local[:3] + [last]:
        c.wait()


def gather(frames, cotangent, wq, wo):
    seq_size, dp_size = lax.axis_size("seq"), lax.axis_size("dp")
    records, frame_count, width = frames.shape
    shard, wide = wo.shape
    anywhere = pl.BlockSpec(memory_space=pl.ANY)
    slab = jax.ShapeDtypeStruct((records, frame_count * seq_size, width), BF)
    dma = pltpu.SemaphoreType.DMA
    return pl.pallas_call(
        functools.partial(gather_kernel, seq_size, dp_size),
        out_shape=(
            slab, slab,
            jax.ShapeDtypeStruct((shard * dp_size, 3 * wide), BF),
            jax.ShapeDtypeStruct((shard * dp_size, wide), BF),
            jax.ShapeDtypeStruct((seq_size, wide, wide), BF),
        ),
        in_specs=[anywhere] * 4,
        out_specs=(anywhere,) * 5,
        scratch_shapes=[
            dma((2, seq_size)), dma((2, seq_size)), dma((3, dp_size)), dma((3, dp_size)),
            dma((seq_size,)), dma((seq_size,)), dma((5,)),
        ],
        compiler_params=pltpu.CompilerParams(collective_id=0, has_side_effects=True),
    )(frames, cotangent, wq, wo)


def dot(a, b, ca=1, cb=0):
    return lax.dot_general(a, b, (((ca,), (cb,)), ((), ())), preferred_element_type=F32)


def core_kernel(
    head_size, lengths, fr, ct, wq, wo, result, norm_part, wq_part, wo_part,
    normed, og, qkv, mgrad, mixed, kv_acc, qkv_grad, wq_acc, wo_acc,
):
    rec = pl.program_id(0)
    slab, width = fr.shape[1:]
    wide = wo.shape[0]
    length = lengths[rec]
    scale = 1.0 / math.sqrt(head_size)
    chunk = min(512, slab)
    pair = min(wide, 128)
    per = pair // head_size
    pad_zero = jnp.zeros((PAD, 3 * wide), BF)
    qkv[pl.ds(0, PAD), :] = pad_zero
    qkv[pl.ds(PAD + slab, PAD), :] = pad_zero
    kv_acc[...] = jnp.zeros_like(kv_acc)

    @pl.when(rec == 0)
    def _():
        wq_acc[...] = jnp.zeros_like(wq_acc)
        wo_acc[...] = jnp.zeros_like(wo_acc)

    @pl.loop(0, slab // BLOCK)
    def _(b):
        rows = pl.ds(pl.multiple_of(b * BLOCK, BLOCK), BLOCK)
        normed[rows, :] = norm_rows(fr[0, rows, :])[0].astype(BF)
        pos = b * BLOCK + lax.broadcasted_iota(jnp.int32, (BLOCK, width), 0)
        og[rows, :] = jnp.where(pos < length, ct[0, rows, :].astype(F32), 0.0).astype(BF)

    @pl.loop(0, slab // chunk)
    def _(b):
        start = pl.multiple_of(b * chunk, chunk)
        rows = pl.ds(start, chunk)
        qkv[pl.ds(PAD + start, chunk), :] = dot(normed[rows, :], wq[...]).astype(BF)
        mgrad[rows, :] = dot(og[rows, :], wo[...], 1, 1).astype(BF)

    @pl.loop(0, slab // BLOCK)
    def _(b):
        start = pl.multiple_of(b * BLOCK, BLOCK)
        rows = pl.ds(start, BLOCK)
        window = pl.ds(start, SPAN)
        shape = (per * BLOCK, SPAN)
        t = start + lax.rem(lax.broadcasted_iota(jnp.int32, shape, 0), BLOCK)
        k = start - PAD + lax.broadcasted_iota(jnp.int32, shape, 1)
        c = t - lax.rem(t, GROUP)
        allowed = (k >= 0) & (k < slab) & (k >= c - LEFT) & (k < c + GROUP + AHEAD)
        allowed = allowed & ((k < length) | (t >= length))
        lane = lax.broadcasted_iota(jnp.int32, (BLOCK, pair), 1) // head_size

        def stack(value):
            if per == 1:
                return value
            value = value.astype(F32)
            return jnp.concatenate(
                [jnp.where(lane == i, value, 0.0) for i in range(per)], axis=0
            ).astype(BF)

        def unstack(value):
            out = value[:BLOCK]
            for i in range(1, per):
                out = jnp.where(lane == i, value[i * BLOCK : (i + 1) * BLOCK], out)
            return out

        for p in range(wide // pair):
            cols = pl.ds(p * pair, pair)
            kcols = pl.ds(wide + p * pair, pair)
            vcols = pl.ds(2 * wide + p * pair, pair)
            q = stack(qkv[pl.ds(PAD + start, BLOCK), cols])
            mg = stack(mgrad[rows, cols])
            keys = qkv[window, kcols]
            values = qkv[window, vcols]
            scores = jnp.where(allowed, dot(q, keys, 1, 1) * scale, -1e30)
            shifted = jnp.exp(scores - jnp.max(scores, axis=-1, keepdims=True))
            shifted = jnp.where(allowed, shifted, 0.0)
            probs = shifted / jnp.sum(shifted, axis=-1, keepdims=True)
            half = probs.astype(BF)
            mixed[rows, cols] = unstack(dot(half, values)).astype(BF)
            pg = dot(mg, values, 1, 1)
            sg = probs * (pg - jnp.sum(probs * pg, axis=-1, keepdims=True)) * scale
            sg = sg.astype(BF)
            qkv_grad[rows, cols] = unstack(dot(sg, keys)).astype(BF)
            kv_acc[window, cols] += dot(sg, q, 0, 0)
            kv_acc[window, kcols] += dot(half, mg, 0, 0)

    @pl.loop(0, slab // chunk)
    def _(b):
        start = pl.multiple_of(b * chunk, chunk)
        rows = pl.ds(start, chunk)
        qkv_grad[rows, pl.ds(wide, 2 * wide)] = kv_acc[pl.ds(PAD + start, chunk), :].astype(BF)
        pos = start + lax.broadcasted_iota(jnp.int32, (chunk, width), 0)
        out = jnp.where(pos < length, dot(mixed[rows, :], wo[...]), 0.0)
        result[0, rows, :] = out.astype(BF)
        norm_part[0, rows, :] = dot(qkv_grad[rows, :], wq[...], 1, 1).astype(BF)
        wq_acc[...] += dot(normed[rows, :], qkv_grad[rows, :], 0, 0)
        wo_acc[...] += dot(mixed[rows, :], og[rows, :], 0, 0)

    @pl.when(rec == pl.num_programs(0) - 1)
    def _():
        wq_part[...] = wq_acc[...].astype(BF)
        for p in range(width // wide):
            wo_part[p] = wo_acc[:, p * wide : (p + 1) * wide].astype(BF)


def core(lengths, fr_all, ct_all, wq_all, wo_rows):
    records, slab, width = fr_all.shape
    wide = wo_rows.shape[0]
    per_rec = pl.BlockSpec((1, slab, width), lambda r: (r, 0, 0))
    wq_spec = pl.BlockSpec((width, 3 * wide), lambda r: (0, 0))
    wo_spec = pl.BlockSpec((wide, width), lambda r: (0, 0))
    rows = jax.ShapeDtypeStruct((records, slab, width), BF)
    return pl.pallas_call(
        functools.partial(core_kernel, width // H),
        grid=(records,),
        out_shape=(
            rows, rows,
            jax.ShapeDtypeStruct((width, 3 * wide), BF),
            jax.ShapeDtypeStruct((width // wide, wide, wide), BF),
        ),
        in_specs=[pl.BlockSpec(memory_space=pltpu.SMEM), per_rec, per_rec, wq_spec, wo_spec],
        out_specs=(
            per_rec, per_rec, wq_spec,
            pl.BlockSpec((width // wide, wide, wide), lambda r: (0, 0, 0)),
        ),
        scratch_shapes=[
            pltpu.VMEM((slab, width), BF),
            pltpu.VMEM((slab, width), BF),
            pltpu.VMEM((slab + 2 * PAD, 3 * wide), BF),
            pltpu.VMEM((slab, wide), BF),
            pltpu.VMEM((slab, wide), BF),
            pltpu.VMEM((slab + 2 * PAD, 2 * wide), F32),
            pltpu.VMEM((slab, 3 * wide), BF),
            pltpu.VMEM((width, 3 * wide), F32),
            pltpu.VMEM((wide, width), F32),
        ],
        compiler_params=pltpu.CompilerParams(vmem_limit_bytes=VMEM_LIMIT),
    )(lengths, fr_all, ct_all, wq_all, wo_rows)


def per_device(frames, lengths, qkv_weight, out_weight, cotangent):
    records, frame_count, model_width = frames.shape
    seq_size = lax.axis_size("seq")
    seq_index = lax.axis_index("seq")
    wide = model_width // seq_size
    shard_rows = qkv_weight.shape[0]
    qkv_mine = lax.dynamic_index_in_dim(
        qkv_weight.reshape(shard_rows, 3, seq_size, wide), seq_index, 2, False
    ).reshape(shard_rows, 3 * wide)
    out_mine = lax.dynamic_slice_in_dim(out_weight, seq_index * wide, wide, 1)
    fr_all, ct_all, wq_all, _, wo_mine = gather(frames, cotangent, qkv_mine, out_mine)
    wo_rows = jnp.swapaxes(wo_mine, 0, 1).reshape(wide, model_width)
    partial, norm_part, part_qkv, part_out = core(lengths, fr_all, ct_all, wq_all, wo_rows)
    return reduce_all(frames, partial, norm_part, part_qkv, part_out, shard_rows)


def reduce_kernel(
    seq_size, dp_size, fr, res_part, norm_part, wq_part, wo_part,
    result, frame_grad, qkv_out, out_out,
    wo_cols, near_r, far_r, near_n, far_n, near_q, far_q, near_o, far_o,
    mine_q, mine_o, got_q, got_o, send_sem, recv_sem, own_sem,
):
    s, j = lax.axis_index("seq"), lax.axis_index("dp")
    records, frame_count, width = fr.shape
    wide = wo_part.shape[1]
    shard = qkv_out.shape[0]
    greet(seq_size, dp_size)
    every = []

    def start(src, dst, to):
        n = len(every)
        c = pltpu.make_async_remote_copy(
            src_ref=src, dst_ref=dst, send_sem=send_sem.at[n], recv_sem=recv_sem.at[n],
            device_id=to, device_id_type=MESH,
        )
        c.start()
        every.append(c)
        return c

    class Hop:
        def __init__(self, block, near, far, me, size, device):
            self.block, self.near, self.far = block, near, far
            self.hi, self.lo, self.his = me // 2, lax.rem(me, 2), size // 2
            self.device = device

        def first(self):
            self.coming = {}
            for d in list(range(1, self.his)) + [0]:
                owner = lax.rem(self.hi + d, self.his) * 2 + 1 - self.lo
                self.coming[d] = start(
                    self.block(owner), self.near.at[d], self.device(self.hi * 2 + 1 - self.lo)
                )

        def second(self):
            self.late = []
            for d in range(1, self.his):
                self.coming[d].wait_recv()
                owner = lax.rem(self.hi + d, self.his) * 2 + self.lo
                own = self.block(owner)
                each_chunk(self.near.at[d], lambda at: put(
                    self.near.at[d], at, self.near.at[d][at].astype(F32) + own[at].astype(F32)
                ))
                self.late.append(start(self.near.at[d], self.far.at[d], self.device(owner)))

        def wait(self):
            self.coming[0].wait_recv()
            for c in self.late:
                c.wait_recv()
            self.own = self.block(self.hi * 2 + self.lo)

        def total(self, at):
            value = self.near.at[0][at].astype(F32) + self.own[at].astype(F32)
            for d in range(1, self.his):
                value = value + self.far.at[d][at].astype(F32)
            return value

    def put(ref, at, value):
        ref[at] = value.astype(ref.dtype)

    def each_chunk(ref, body):
        if len(ref.shape) == 3:
            for r in range(ref.shape[0]):
                @pl.loop(0, ref.shape[1] // 32)
                def _(b):
                    body((r, pl.ds(pl.multiple_of(b * 32, 32), 32)))
        else:
            @pl.loop(0, ref.shape[0] // 32)
            def _(b):
                body((pl.ds(pl.multiple_of(b * 32, 32), 32),))

    on_dp = lambda i: (i, s)
    on_seq = lambda i: (j, i)
    frame_block = lambda ref: lambda i: ref.at[:, pl.ds(i * frame_count, frame_count)]
    row_block = lambda ref: lambda i: ref.at[pl.ds(i * shard, shard)]
    hop_q = Hop(row_block(wq_part), near_q, far_q, j, dp_size, on_dp)
    hop_o = Hop(row_block(wo_cols), near_o, far_o, j, dp_size, on_dp)
    hop_n = Hop(frame_block(norm_part), near_n, far_n, s, seq_size, on_seq)
    hop_r = Hop(frame_block(res_part), near_r, far_r, s, seq_size, on_seq)

    swaps = []
    hop_q.first()
    for d in range(1, seq_size):
        to = lax.rem(s + d, seq_size)
        swaps.append(start(wo_part.at[to], wo_cols.at[pl.ds(s * wide, wide)], on_seq(to)))
    own = pltpu.make_async_copy(wo_part.at[s], wo_cols.at[pl.ds(s * wide, wide)], own_sem)
    own.start()
    hop_n.first()
    hop_r.first()
    hop_n.second()
    own.wait()
    for c in swaps:
        c.wait_recv()
    hop_o.first()
    hop_q.second()
    hop_o.second()
    hop_r.second()

    hop_n.wait()

    def normalise(at):
        centred, inv_std = norm_rows(fr[at])
        grad = hop_n.total(at)
        one = jnp.mean(grad, axis=-1, keepdims=True)
        two = jnp.mean(grad * centred, axis=-1, keepdims=True)
        frame_grad[at] = ((grad - one - centred * two) * inv_std).astype(BF)

    each_chunk(fr, normalise)

    hop_q.wait()
    each_chunk(mine_q, lambda at: put(mine_q, at, hop_q.total(at)))
    hop_o.wait()
    each_chunk(mine_o, lambda at: put(mine_o, at, hop_o.total(at)))
    outer, core_id, outers = s // 2, lax.rem(s, 2), seq_size // 2
    beside = on_seq(outer * 2 + 1 - core_id)
    arrivals, near = {}, []
    for d in range(1, outers):
        to = on_seq(lax.rem(outer + d, outers) * 2 + core_id)
        arrivals[d] = (start(mine_q, got_q.at[s], to), start(mine_o, got_o.at[s], to))
    near += [start(mine_q, got_q.at[s], beside), start(mine_o, got_o.at[s], beside)]

    hop_r.wait()
    each_chunk(result, lambda at: put(result, at, hop_r.total(at)))

    local = [
        pltpu.make_async_copy(mine_q, got_q.at[s], own_sem),
        pltpu.make_async_copy(mine_o, got_o.at[s], own_sem),
    ]
    for c in local:
        c.start()
        c.wait()
    for d, pair in arrivals.items():
        owner = lax.rem(outer + outers - d, outers) * 2 + core_id
        for c, got in zip(pair, (got_q, got_o)):
            c.wait_recv()
            near.append(start(got.at[owner], got.at[owner], beside))
    for c in near:
        c.wait_recv()
    for p in range(seq_size):
        for k in range(3):
            qkv_out[:, k * width + p * wide : k * width + (p + 1) * wide] = got_q[
                p, :, k * wide : (k + 1) * wide
            ].astype(F32)
        out_out[:, p * wide : (p + 1) * wide] = got_o[p].astype(F32)
    for c in every:
        c.wait_send()


def reduce_all(frames, partial, norm_part, part_qkv, part_out, shard):
    records, frame_count, width = frames.shape
    seq_size, dp_size = lax.axis_size("seq"), lax.axis_size("dp")
    wide = width // seq_size
    vmem = pl.BlockSpec(memory_space=pltpu.VMEM)
    outers, zeds = seq_size // 2, dp_size // 2
    act = pltpu.VMEM((outers, records, frame_count, width), BF)
    wq = pltpu.VMEM((zeds, shard, 3 * wide), BF)
    wo = pltpu.VMEM((zeds, shard, wide), BF)
    copies = 4 * (seq_size + dp_size) + 3 * seq_size
    return pl.pallas_call(
        functools.partial(reduce_kernel, seq_size, dp_size),
        out_shape=(
            jax.ShapeDtypeStruct(frames.shape, BF),
            jax.ShapeDtypeStruct(frames.shape, BF),
            jax.ShapeDtypeStruct((shard, 3 * width), F32),
            jax.ShapeDtypeStruct((shard, width), F32),
        ),
        in_specs=[vmem] * 5,
        out_specs=(vmem,) * 4,
        scratch_shapes=[
            pltpu.VMEM((width, wide), BF),
            act, act, act, act, wq, wq, wo, wo,
            pltpu.VMEM((shard, 3 * wide), BF),
            pltpu.VMEM((shard, wide), BF),
            pltpu.VMEM((seq_size, shard, 3 * wide), BF),
            pltpu.VMEM((seq_size, shard, wide), BF),
            pltpu.SemaphoreType.DMA((copies,)),
            pltpu.SemaphoreType.DMA((copies,)),
            pltpu.SemaphoreType.DMA,
        ],
        compiler_params=pltpu.CompilerParams(
            collective_id=1, has_side_effects=True, vmem_limit_bytes=VMEM_LIMIT
        ),
    )(frames, partial, norm_part, part_qkv, part_out)


def solution(mesh):
    in_specs = (P("dp", "seq", None), P("dp"), P("dp", None), P("dp", None), P("dp", "seq", None))
    out_specs = (P("dp", "seq", None), P("dp", "seq", None), P("dp", None), P("dp", None))
    return jax.shard_map(
        per_device, mesh=mesh, in_specs=in_specs, out_specs=out_specs, check_vma=False
    )
```
